512 devices in a mesh: head: 8 (over y_lo, x), blk: 64 (over z, y_hi, core).
Axes of the slice: x: 4, y: 4 (y_hi: 2, y_lo: 2; y = y_hi * 2 + y_lo), z: 16, core: 2. Of those that a mesh axis runs over, the one named last changes fastest.
Arguments:
- query_rows: bfloat16 [32768, 2048], P(('blk', 'head')), may hold values from -128 to 128, as said below
- key_rows: bfloat16 [32768, 2048], P(('blk', 'head')), may hold values from -4 to 4
- value_rows: bfloat16 [32768, 2048], P(('blk', 'head')), may hold values from -6 to 6
- grad_out: bfloat16 [32768, 2048], P(('blk', 'head')), may hold values from -6 to 6
Outputs:
- attended: bfloat16 [32768, 2048], P(('blk', 'head'))
- grad_query: bfloat16 [32768, 2048], P(('blk', 'head'))
- grad_key: bfloat16 [32768, 2048], P(('blk', 'head'))
- grad_value: bfloat16 [32768, 2048], P(('blk', 'head'))
The draws below stay inside these ranges and needn't reach their ends.
Inputs may be any that keep to these rules, and one draw needn't show every extreme that they name: `query_rows`: a few query rows may be large, with scores up to about 300.
All inputs are finite; a program needn't handle non-finite values.
Results may differ from the reference program's by a relative error of at most 0.035.
Values may be sent and summed in bfloat16 or wider, within the bound.
A program may use at most 64 MiB of HBM per device.

```python
import math
import jax
import jax.numpy as jnp
from jax import lax

HEADS = 16
DH = 128
TOKENS = 32768
N_BLK = 64


def shared_keys(key):
    return jnp.clip(jax.random.normal(key, (TOKENS, HEADS * DH), jnp.float32), -4.0, 4.0)


def draw_key_rows(key, part):
    base = shared_keys(key)
    return base.astype(jnp.bfloat16)


def draw_query_rows(key, part):
    key = jax.random.fold_in(key, 12)
    drawn = jnp.clip(jax.random.normal(key, (TOKENS, HEADS * DH), jnp.float32), -4.0, 4.0)
    return drawn.astype(jnp.bfloat16)


def block_levels(key, extent, split, smallest, largest):
    factor_of = 1.0
    for dim, blocks in split:
        steps = jax.random.uniform(jax.random.fold_in(jax.random.fold_in(key, 6), dim), (blocks,), jnp.float32, smallest / len(split), largest / len(split))
        factor_of = factor_of * jnp.repeat(jnp.exp(steps), extent[dim] // blocks).reshape((-1,) + (1,) * (len(extent) - 1 - dim))
    return factor_of


def bell_draw(key, shape, spread, reach, cuts=(), held_as=jnp.bfloat16):
    entries = spread * jax.random.normal(key, shape, jnp.float32)
    if cuts:
        entries = entries * block_levels(key, shape, cuts, -0.22, 0.18)
    return jnp.clip(entries, -reach, reach).astype(held_as)


def setup_inputs(seed: int = 0) -> dict:
    streams_of = jax.random.split(jax.random.key(seed), 5)
    return {
        "query_rows": draw_query_rows(jax.random.fold_in(streams_of[4], 71), 0),
        "key_rows": draw_key_rows(jax.random.fold_in(streams_of[4], 71), 0),
        "value_rows": bell_draw(streams_of[2], (TOKENS, HEADS * DH), 1.0, 6.0, ((0, 512),)),
        "grad_out": bell_draw(streams_of[3], (TOKENS, HEADS * DH), 1.0, 6.0, ((0, 512),)),
    }


def window(blocks, block):
    count = blocks.shape[0]
    lower = ((block + count - 1) % count).astype(jnp.int32)
    upper = ((block + 1) % count).astype(jnp.int32)
    return jnp.concatenate([blocks[lower], blocks[block], blocks[upper]], axis=0)

def window_valid(block, seg_rows):
    lower_ok = jnp.full((seg_rows,), block > 0)
    middle = jnp.full((seg_rows,), True)
    upper_ok = jnp.full((seg_rows,), block < N_BLK - 1)
    return jnp.concatenate([lower_ok, middle, upper_ok], axis=0)

def rounded(values):
    return lax.optimization_barrier(values.astype(jnp.bfloat16)).astype(jnp.float32)

def reference(query_rows, key_rows, value_rows, grad_out):
    seg_rows = TOKENS // N_BLK
    scaling = 1.0 / math.sqrt(DH)
    block_shape = (N_BLK, seg_rows, HEADS, DH)
    query_blocks = query_rows.reshape(block_shape)
    key_blocks = key_rows.reshape(block_shape)
    value_blocks = value_rows.reshape(block_shape)
    grad_blocks = grad_out.reshape(block_shape)

    def forward_pass(block):
        queries = query_blocks[block].astype(jnp.float32)
        window_keys = window(key_blocks, block).astype(jnp.float32)
        window_values = window(value_blocks, block).astype(jnp.float32)
        grads = grad_blocks[block].astype(jnp.float32)
        valid = window_valid(block, seg_rows)
        scores = jnp.einsum('qhd,khd->hqk', queries, window_keys) * scaling
        scores = jnp.where(valid[None, None, :], scores, -jnp.inf)
        row_top = lax.optimization_barrier(jnp.max(scores, axis=2, keepdims=True))
        log_total = row_top + jnp.log(lax.optimization_barrier(jnp.sum(jnp.exp(scores - row_top), axis=2, keepdims=True)))
        probs = jnp.exp(scores - log_total)
        probs_low = rounded(probs)
        attended = jnp.einsum('hqk,khd->qhd', probs_low, window_values).astype(jnp.bfloat16)
        deltas = lax.optimization_barrier(jnp.sum(grads * attended.astype(jnp.float32), axis=2))
        dprobs = jnp.einsum('qhd,khd->hqk', grads, window_values)
        dscores = rounded(probs * (dprobs - deltas.T[:, :, None]) * scaling)
        grad_query = jnp.einsum('hqk,khd->qhd', dscores, window_keys).astype(jnp.bfloat16)
        return (attended, grad_query, log_total[:, :, 0].T, deltas)
    attended, grad_query, log_totals, delta_table = lax.map(forward_pass, jnp.arange(N_BLK, dtype=jnp.int32))

    def key_pass(block):
        window_queries = window(query_blocks, block).astype(jnp.float32)
        window_grads = window(grad_blocks, block).astype(jnp.float32)
        window_totals = window(log_totals, block)
        window_deltas = window(delta_table, block)
        own_keys = key_blocks[block].astype(jnp.float32)
        own_values = value_blocks[block].astype(jnp.float32)
        valid = window_valid(block, seg_rows)
        scores = jnp.einsum('qhd,khd->hqk', window_queries, own_keys) * scaling
        exponent = jnp.where(valid[None, :, None], scores - window_totals.T[:, :, None], -jnp.inf)
        probs = jnp.exp(exponent)
        probs_low = rounded(probs)
        dprobs = jnp.einsum('qhd,khd->hqk', window_grads, own_values)
        dscores = rounded(probs * (dprobs - window_deltas.T[:, :, None]) * scaling)
        grad_key = jnp.einsum('hqk,qhd->khd', dscores, window_queries).astype(jnp.bfloat16)
        grad_value = jnp.einsum('hqk,qhd->khd', probs_low, window_grads).astype(jnp.bfloat16)
        return (grad_key, grad_value)
    grad_key, grad_value = lax.map(key_pass, jnp.arange(N_BLK, dtype=jnp.int32))
    full_shape = (TOKENS, HEADS * DH)
    return (attended.reshape(full_shape), grad_query.reshape(full_shape), grad_key.reshape(full_shape), grad_value.reshape(full_shape))
```

```python
import math

import jax
import jax.numpy as jnp
from jax import lax
from jax.experimental import pallas as pl
from jax.experimental.pallas import tpu as pltpu
from jax.sharding import PartitionSpec as P

DH = 128
WIDE = 2 * DH
SEG = 512
ROWS = 64
Q_ROWS = 128
SCALE = 1.0 / math.sqrt(DH)
SCALE_2 = SCALE * math.log2(math.e)
BF16 = jnp.bfloat16
F32 = jnp.float32
MESH = pl.DeviceIdType.MESH
PEERS = ((0, 2), (1, 2), (1, 1), (0, 1), (1, 3), (0, 3), (1, 0))
PIECE = 128


def nt(lhs, rhs):
    return lax.dot_general(lhs, rhs, (((1,), (1,)), ((), ())), preferred_element_type=F32)


def nn(lhs, rhs):
    return lax.dot_general(lhs, rhs, (((1,), (0,)), ((), ())), preferred_element_type=F32)


def kernel(
    q_in, k_in, v_in, g_in, att_out, dq_out, dk_out, dv_out,
    kw, vw, q_s, g_s, e_s, d_s, gp_s, att_st, dq_st, dk_st, dv_st, own_k, own_v, t_send, t_recv,
    in_send, in_recv, halo_send, halo_recv, term_send, term_recv, out_send, out_recv,
):
    head = lax.axis_index("head")
    blk = lax.axis_index("blk")
    count = lax.axis_size("blk")
    y_hi = (blk // 2) % 2
    core = blk % 2
    mine = (head + 4 * y_hi) % 8
    peers = [((head // 4 + dy) % 2) * 4 + (head % 4 + dx) % 4 for dy, dx in PEERS]
    across = (head + 4) % 8
    up = {"blk": (blk + 1) % count, "head": core * across + (1 - core) * head}
    down = {"blk": (blk + count - 1) % count, "head": core * head + (1 - core) * across}
    has_lower = blk > 0
    has_upper = blk < count - 1

    def remote(src, dst, send, recv, target):
        copy = pltpu.make_async_remote_copy(
            src_ref=src, dst_ref=dst, send_sem=send, recv_sem=recv, device_id=target, device_id_type=MESH
        )
        copy.start()

    def settle(ref, sem):
        pltpu.make_async_copy(ref, ref, sem).wait()

    barrier = pltpu.get_barrier_semaphore()
    for target in [{"head": p} for p in peers] + [up, down]:
        pl.semaphore_signal(barrier, inc=1, device_id=target, device_id_type=MESH)
    pl.semaphore_wait(barrier, len(peers) + 2)

    my_rows = pl.ds(pl.multiple_of(head * ROWS, ROWS), ROWS)

    def spread(src, landing, start, width, send, recv):
        for p in peers:
            column = pl.multiple_of(((p + 4 * y_hi) % 8) * WIDE + start, DH)
            remote(src.at[:, pl.ds(column, width)], landing, send, recv, {"head": p})
        column = pl.multiple_of(mine * WIDE + start, DH)
        pltpu.make_async_copy(src.at[:, pl.ds(column, width)], landing, recv).start()

    spread(k_in, kw.at[1, my_rows, :], 0, WIDE, in_send.at[0], in_recv.at[0])
    spread(v_in, vw.at[1, my_rows, :], 0, WIDE, in_send.at[1], in_recv.at[1])
    for hd in range(2):
        spread(q_in, q_s.at[hd, my_rows, :], hd * DH, DH, in_send.at[2 + 2 * hd], in_recv.at[2 + 2 * hd])
        spread(g_in, g_s.at[hd, my_rows, :], hd * DH, DH, in_send.at[3 + 2 * hd], in_recv.at[3 + 2 * hd])

    for n, window in enumerate((kw, vw)):
        settle(window.at[1], in_recv.at[n])
        for hd in range(2):
            cols = pl.ds(hd * DH, DH)
            for r in range(0, SEG, PIECE):
                rows = pl.ds(r, PIECE)
                remote(window.at[1, rows, cols], window.at[0, rows, cols],
                       halo_send.at[n, hd, 0], halo_recv.at[n, hd, 0], up)
                remote(window.at[1, rows, cols], window.at[2, rows, cols],
                       halo_send.at[n, hd, 1], halo_recv.at[n, hd, 1], down)

    factors = [jnp.where(has_lower, SCALE_2, 0.0), SCALE_2, jnp.where(has_upper, SCALE_2, 0.0)]

    def collect(staged, out, n, hd):
        for p in peers:
            rows = pl.ds(pl.multiple_of(p * ROWS, ROWS), ROWS)
            column = pl.multiple_of(mine * WIDE + hd * DH, DH)
            remote(staged.at[hd, rows, :], out.at[:, pl.ds(column, DH)],
                   out_send.at[n, hd], out_recv.at[n], {"head": p})
        column = pl.multiple_of(mine * WIDE + hd * DH, DH)
        pltpu.make_async_copy(staged.at[hd, my_rows, :], out.at[:, pl.ds(column, DH)], out_recv.at[n]).start()

    def attend(hd):
        cols = pl.ds(hd * DH, DH)
        for r in range(0, SEG, Q_ROWS):
            rows = pl.ds(r, Q_ROWS)
            query = q_s[hd, rows, :]
            scores = [nt(query, kw[j, :, cols]) for j in range(3)]
            tops = [jnp.max(s, axis=1, keepdims=True) for s in scores]
            top = jnp.maximum(
                jnp.maximum(jnp.where(has_lower, tops[0], -jnp.inf), tops[1]),
                jnp.where(has_upper, tops[2], -jnp.inf),
            ) * SCALE_2
            shifts = [jnp.where(has_lower, top, 1e30), top, jnp.where(has_upper, top, 1e30)]
            total = 0.0
            attended = 0.0
            for j in range(3):
                e = jnp.exp2(scores[j] * factors[j] - shifts[j])
                total = total + jnp.sum(e, axis=1, keepdims=True)
                low = e.astype(BF16)
                e_s[j, rows, :] = low
                attended = attended + nn(low, vw[j, :, cols])
            inverse = 1.0 / total
            attended = attended * inverse
            att_st[hd, rows, :] = attended.astype(BF16)
            scaled = (g_s[hd, rows, :].astype(F32) * (inverse * SCALE)).astype(BF16)
            gp_s[rows, :] = scaled
            delta = jnp.sum(scaled.astype(F32) * attended, axis=1, keepdims=True)
            for j in range(3):
                dprobs = nt(scaled, vw[j, :, cols])
                d_s[j, rows, :] = (dprobs - delta).astype(BF16) * e_s[j, rows, :]

    def send_term(n, hd, side):
        target = down if side == 0 else up
        for r in range(0, SEG, PIECE):
            rows = pl.ds(r, PIECE)
            remote(t_send.at[n, hd, side, rows, :], t_recv.at[n, hd, 1 - side, rows, :],
                   term_send.at[n, hd, side], term_recv.at[n, hd, 1 - side], target)

    def backward(hd):
        cols = pl.ds(hd * DH, DH)
        grads_t = gp_s[...].T
        queries_t = q_s[hd].T
        for side in range(2):
            t_send[1, hd, side] = (nn(grads_t, e_s[2 * side]) * (1.0 / SCALE)).T.astype(BF16)
            send_term(1, hd, side)
        for side in range(2):
            t_send[0, hd, side] = nn(queries_t, d_s[2 * side]).T.astype(BF16)
            send_term(0, hd, side)
        own_v[hd] = (nn(grads_t, e_s[1]) * (1.0 / SCALE)).T
        own_k[hd] = nn(queries_t, d_s[1]).T
        for r in range(0, SEG, Q_ROWS):
            rows = pl.ds(r, Q_ROWS)
            dq_st[hd, rows, :] = (
                nn(d_s[0, rows, :], kw[0, :, cols]) + nn(d_s[1, rows, :], kw[1, :, cols])
                + nn(d_s[2, rows, :], kw[2, :, cols])
            ).astype(BF16)

    def finish(hd):
        for n, own, staged, out in ((1, own_v, dv_st, dv_out), (0, own_k, dk_st, dk_out)):
            for side in range(2):
                settle(t_recv.at[n, hd, side], term_recv.at[n, hd, side])
            staged[hd] = (
                own[hd] + t_recv[n, hd, 0].astype(F32) + t_recv[n, hd, 1].astype(F32)
            ).astype(BF16)
            collect(staged, out, 2 + n, hd)

    for hd in range(2):
        cols = pl.ds(hd * DH, DH)
        settle(q_s.at[hd], in_recv.at[2 + 2 * hd])
        settle(g_s.at[hd], in_recv.at[3 + 2 * hd])
        for n, window in enumerate((kw, vw)):
            settle(window.at[0, :, cols], halo_recv.at[n, hd, 0])
            settle(window.at[2, :, cols], halo_recv.at[n, hd, 1])
        attend(hd)
        collect(att_st, att_out, 0, hd)
        if hd == 1:
            finish(0)
        backward(hd)
        collect(dq_st, dq_out, 1, hd)
    finish(1)

    for n, out in enumerate((att_out, dq_out, dk_out, dv_out)):
        settle(out, out_recv.at[n])
    seven = pl.ds(0, 7 * ROWS)
    settle(kw.at[1, seven, :], in_send.at[0])
    settle(vw.at[1, seven, :], in_send.at[1])
    for hd in range(2):
        cols = pl.ds(hd * DH, DH)
        settle(q_s.at[hd, seven, :], in_send.at[2 + 2 * hd])
        settle(g_s.at[hd, seven, :], in_send.at[3 + 2 * hd])
        for n, window in enumerate((kw, vw)):
            for side in range(2):
                settle(window.at[1, :, cols], halo_send.at[n, hd, side])
                settle(t_send.at[n, hd, side], term_send.at[n, hd, side])
        for n, staged in enumerate((att_st, dq_st, dk_st, dv_st)):
            settle(staged.at[hd, seven, :], out_send.at[n, hd])


def on_device(query_rows, key_rows, value_rows, grad_out):
    dma = pltpu.SemaphoreType.DMA
    seg_half = pltpu.VMEM((2, SEG, DH), BF16)
    seg_full = pltpu.VMEM((2, SEG, DH), F32)
    out = jax.ShapeDtypeStruct(query_rows.shape, BF16)
    return pl.pallas_call(
        kernel,
        out_shape=[out] * 4,
        in_specs=[pl.BlockSpec(memory_space=pltpu.HBM)] * 4,
        out_specs=[pl.BlockSpec(memory_space=pltpu.HBM)] * 4,
        scratch_shapes=[
            pltpu.VMEM((3, SEG, WIDE), BF16),
            pltpu.VMEM((3, SEG, WIDE), BF16),
            seg_half,
            seg_half,
            pltpu.VMEM((3, SEG, SEG), BF16),
            pltpu.VMEM((3, SEG, SEG), BF16),
            pltpu.VMEM((SEG, DH), BF16),
            seg_half,
            seg_half,
            seg_half,
            seg_half,
            seg_full,
            seg_full,
            pltpu.VMEM((2, 2, 2, SEG, DH), BF16),
            pltpu.VMEM((2, 2, 2, SEG, DH), BF16),
            dma((6,)),
            dma((6,)),
            dma((2, 2, 2)),
            dma((2, 2, 2)),
            dma((2, 2, 2)),
            dma((2, 2, 2)),
            dma((4, 2)),
            dma((4,)),
        ],
        compiler_params=pltpu.CompilerParams(
            collective_id=0, has_side_effects=True, vmem_limit_bytes=63 * 2**20
        ),
        cost_estimate=pl.CostEstimate(flops=2_400_000_000, bytes_accessed=2 * 2**20, transcendentals=1_600_000),
        name="window_attention",
    )(query_rows, key_rows, value_rows, grad_out)


def solution(mesh):
    spec = P(("blk", "head"), None)
    return jax.shard_map(
        on_device, mesh=mesh, in_specs=(spec,) * 4, out_specs=(spec,) * 4, check_vma=False
    )
```

```python
import math

import jax
import jax.numpy as jnp
from jax import lax
from jax.experimental import pallas as pl
from jax.experimental.pallas import tpu as pltpu
from jax.sharding import PartitionSpec as P

DH = 128
HEADS = 16
SEG = 512
ROWS = 64
Q_ROWS = 128
SCALE = 1.0 / math.sqrt(DH)
SCALE_2 = SCALE * math.log2(math.e)
BF16 = jnp.bfloat16
F32 = jnp.float32
MESH = pl.DeviceIdType.MESH
PLANE = (
    (2, 2), (2, 1), (1, 2), (2, 3), (3, 2), (1, 1), (3, 3), (1, 3), (3, 1),
    (0, 2), (2, 0), (0, 1), (1, 0), (0, 3), (3, 0), (0, 0),
)
OWNERS = ((1, 2), (0, 2), (1, 1), (1, 3), (0, 1), (0, 3), (1, 0), (0, 0))


def nt(lhs, rhs):
    return lax.dot_general(lhs, rhs, (((1,), (1,)), ((), ())), preferred_element_type=F32)


def nn(lhs, rhs):
    return lax.dot_general(lhs, rhs, (((1,), (0,)), ((), ())), preferred_element_type=F32)


def kernel(
    q_in, k_in, v_in, g_in, att_out, dq_out, dk_out, dv_out,
    staged_in, landed, kw, vw, q_s, g_s, e_s, d_s, gp_s, att_f, inv_s, att_st, dq_st, dk_st, dv_st,
    t_send, t_recv, stage_sem, store_sem,
    in_send, in_recv, halo_send, halo_recv, term_send, term_recv, out_send, out_recv,
):
    head = lax.axis_index("head")
    blk = lax.axis_index("blk")
    planes = lax.axis_size("blk") // 4
    z, y_hi, core = blk // 4, (blk // 2) % 2, blk % 2
    y_lo, x = head // 4, head % 4
    y = 2 * y_hi + y_lo
    mine = 4 * y + x
    away = (y_hi + core) % 2
    at_home = away == 0
    at_end = jnp.where(z + core == 0, 1, 0) + jnp.where(z + core == planes, 1, 0)
    has_far = at_end == 0
    far = {"blk": blk - 3 + 6 * core, "head": head}
    near = {"blk": blk + 1 - 2 * core, "head": head}
    segs = (core, 1 - core)

    def remote(src, dst, send, recv, target):
        pltpu.make_async_remote_copy(
            src_ref=src, dst_ref=dst, send_sem=send, recv_sem=recv, device_id=target, device_id_type=MESH
        ).start()

    def settle(ref, sem):
        pltpu.make_async_copy(ref, ref, sem).wait()

    def owners(turn):
        for dy, dx in OWNERS:
            there = ((y_lo + dy) % 2) * 4 + (x + dx) % 4
            yield {"blk": 4 * z + 2 * core + segs[turn], "head": there}, there, turn == 0 and (dy, dx) == (0, 0)

    inputs = (k_in, v_in, q_in, g_in)
    staging = [pltpu.make_async_copy(src, staged_in.at[n], stage_sem.at[n]) for n, src in enumerate(inputs)]
    for copy in staging:
        copy.start()
    barrier = pltpu.get_barrier_semaphore()

    def greet(target):
        pl.semaphore_signal(barrier, inc=1, device_id=target, device_id_type=MESH)

    pl.when(has_far)(lambda: greet(far))
    greet(near)
    for turn in range(2):
        for target, _, own in owners(turn):
            if own:
                pl.when(jnp.logical_not(at_home))(lambda target=target: greet(target))
            else:
                greet(target)

    @pl.when(jnp.logical_not(has_far))
    def _():
        kw[3 * core] = jnp.zeros((SEG, DH), BF16)
        vw[3 * core] = jnp.zeros((SEG, DH), BF16)
        t_recv[0, 0] = jnp.zeros((SEG, DH), BF16)
        t_recv[1, 0] = jnp.zeros((SEG, DH), BF16)

    pl.semaphore_wait(barrier, 17 + away - at_end)

    my_rows = pl.ds(pl.multiple_of(head * ROWS, ROWS), ROWS)
    my_column = pl.ds(pl.multiple_of(mine * DH, DH), DH)

    def spread(n, landing):
        send, recv = in_send.at[n], in_recv.at[n, away]
        staging[n].wait()
        for dy, dx in PLANE:
            there_y, there_x = (y + dy) % 4, (x + dx) % 4
            columns = pl.ds(pl.multiple_of((4 * there_y + there_x) * DH, DH), DH)
            target = {"blk": 4 * z + 2 * (there_y // 2) + y_hi, "head": (there_y % 2) * 4 + there_x}

            def go(columns=columns, target=target):
                remote(staged_in.at[n, :, columns], landing, send, recv, target)

            if (dy, dx) == (0, 0):
                pl.when(jnp.logical_not(at_home))(go)

                @pl.when(at_home)
                def _():
                    pltpu.make_async_copy(inputs[n].at[:, my_column], landing, recv).start()
            else:
                go()

    spread(0, kw.at[1 + core, my_rows, :])
    spread(1, vw.at[1 + core, my_rows, :])
    spread(2, q_s.at[away, my_rows, :])
    spread(3, g_s.at[away, my_rows, :])

    for n, window in enumerate((kw, vw)):
        settle(window.at[1 + core], in_recv.at[n, 0])
        pl.when(has_far)(lambda n=n, window=window: remote(
            window.at[1 + core], window.at[3 - 3 * core], halo_send.at[n, 0], halo_recv.at[n, 0], far
        ))
        settle(window.at[2 - core], in_recv.at[n, 1])
        remote(window.at[2 - core], window.at[3 * core], halo_send.at[n, 1], halo_recv.at[n, 1], near)

    def collect(staged, n, turn):
        for target, there, own in owners(turn):
            rows = pl.ds(pl.multiple_of(there * ROWS, ROWS), ROWS)

            def go(rows=rows, target=target):
                remote(staged.at[turn, rows, :], landed.at[n, :, my_column], out_send.at[n], out_recv.at[n], target)

            if own:
                pl.when(jnp.logical_not(at_home))(go)

                @pl.when(at_home)
                def _():
                    landed[n, :, my_column] = staged[turn, my_rows, :]
            else:
                go()

    def attend(turn):
        seg = segs[turn]
        inside = (True, True, True)
        if turn == 0:
            inside = (core + (1 - at_end) > 0, True, 1 - core + (1 - at_end) > 0)
        factors = [SCALE_2 if ok is True else jnp.where(ok, SCALE_2, 0.0) for ok in inside]
        for r in range(0, SEG, Q_ROWS):
            rows = pl.ds(r, Q_ROWS)
            query = q_s[turn, rows, :]
            scores = [nt(query, kw[seg + j]) for j in range(3)]
            tops = [jnp.max(s, axis=1, keepdims=True) for s in scores]
            tops = [t if ok is True else jnp.where(ok, t, -jnp.inf) for t, ok in zip(tops, inside)]
            top = jnp.maximum(jnp.maximum(tops[0], tops[1]), tops[2]) * SCALE_2
            total = 0.0
            attended = 0.0
            for j in range(3):
                shift = top if inside[j] is True else jnp.where(inside[j], top, 1e30)
                e = jnp.exp2(scores[j] * factors[j] - shift)
                total = total + jnp.sum(e, axis=1, keepdims=True)
                low = e.astype(BF16)
                e_s[turn, j, rows, :] = low
                attended = attended + nn(low, vw[seg + j])
            inverse = 1.0 / total
            attended = attended * inverse
            att_st[turn, rows, :] = attended.astype(BF16)
            att_f[turn, rows, :] = attended
            inv_s[turn, rows, :] = inverse * SCALE

    def score_grads(turn):
        seg = segs[turn]
        for r in range(0, SEG, Q_ROWS):
            rows = pl.ds(r, Q_ROWS)
            scaled = (g_s[turn, rows, :].astype(F32) * inv_s[turn, rows, :]).astype(BF16)
            gp_s[turn, rows, :] = scaled
            delta = jnp.sum(scaled.astype(F32) * att_f[turn, rows, :], axis=1, keepdims=True)
            for j in range(3):
                dprobs = nt(scaled, vw[seg + j])
                d_s[turn, j, rows, :] = (dprobs - delta).astype(BF16) * e_s[turn, j, rows, :]

    def query_grads(turn):
        seg = segs[turn]
        for r in range(0, SEG, Q_ROWS):
            rows = pl.ds(r, Q_ROWS)
            dq_st[turn, rows, :] = sum(nn(d_s[turn, j, rows, :], kw[seg + j]) for j in range(3)).astype(BF16)

    def value_terms(pairs):
        return (sum(nn(gp_s[turn].T, e_s[turn, j]) for turn, j in pairs) * (1.0 / SCALE)).T

    def key_terms(pairs):
        return sum(nn(q_s[turn].T, d_s[turn, j]) for turn, j in pairs).T

    def send_terms(turn):
        outer = (2 * core, 2 - 2 * core)[turn]
        for n, terms in ((1, value_terms), (0, key_terms)):
            t_send[n, turn] = terms([(turn, outer)]).astype(BF16)

            def go(n=n):
                remote(t_send.at[n, turn], t_recv.at[n, turn], term_send.at[n, turn], term_recv.at[n, turn], (far, near)[turn])

            if turn == 0:
                pl.when(has_far)(go)
            else:
                go()

    def finish(turn):
        across = (2 * core, 2 - 2 * core)[turn]
        for n, terms, staged in ((1, value_terms, dv_st), (0, key_terms, dk_st)):
            own = terms([(turn, 1), (1 - turn, across)])

            def arrive(n=n):
                settle(t_recv.at[n, turn], term_recv.at[n, turn])

            if turn == 0:
                pl.when(has_far)(arrive)
            else:
                arrive()
            staged[turn] = (own + t_recv[n, turn].astype(F32)).astype(BF16)
            collect(staged, 2 + n, turn)

    for turn in (1, 0):
        settle(q_s.at[turn], in_recv.at[2, turn])
        for n, window in enumerate((kw, vw)):
            if turn == 0:
                pl.when(has_far)(lambda n=n, window=window: settle(window.at[3 * core], halo_recv.at[n, 0]))
            else:
                settle(window.at[3 - 3 * core], halo_recv.at[n, 1])
        attend(turn)
        collect(att_st, 0, turn)
    for turn in range(2):
        settle(g_s.at[turn], in_recv.at[3, turn])
        score_grads(turn)
        send_terms(turn)
        query_grads(turn)
        collect(dq_st, 1, turn)
    finish(0)
    finish(1)

    storing = [
        pltpu.make_async_copy(landed.at[n], out, store_sem.at[n])
        for n, out in enumerate((att_out, dq_out, dk_out, dv_out))
    ]
    most = pl.ds(0, 15 * DH)

    def settle_chunks(n, sem):
        pl.when(at_home)(lambda: settle(landed.at[n, :, most], sem))
        pl.when(jnp.logical_not(at_home))(lambda: settle(landed.at[n], sem))

    for n in (0, 1, 3, 2):
        settle_chunks(n, out_recv.at[n])
        storing[n].start()
    for n in range(4):
        settle_chunks(n, in_send.at[n])
        settle_chunks(n, out_send.at[n])
    for n in range(2):
        pl.when(has_far)(lambda n=n: settle(kw.at[0], halo_send.at[n, 0]))
        settle(kw.at[0], halo_send.at[n, 1])
        pl.when(has_far)(lambda n=n: settle(t_send.at[n, 0], term_send.at[n, 0]))
        settle(t_send.at[n, 1], term_send.at[n, 1])
    for copy in storing:
        copy.wait()


def handover(*refs):
    sources, results, held, read_sem, write_sem = refs[:4], refs[4:8], refs[8], refs[9], refs[10]
    reads = [pltpu.make_async_copy(src, held.at[n], read_sem.at[n]) for n, src in enumerate(sources)]
    writes = [pltpu.make_async_copy(held.at[n], dst, write_sem.at[n]) for n, dst in enumerate(results)]
    for copy in reads:
        copy.start()
    for read, write in zip(reads, writes):
        read.wait()
        write.start()
    for copy in writes:
        copy.wait()


def on_device(query_rows, key_rows, value_rows, grad_out):
    dma = pltpu.SemaphoreType.DMA
    rows = pltpu.VMEM((4, ROWS, HEADS * DH), BF16)
    window = pltpu.VMEM((4, SEG, DH), BF16)
    pair = pltpu.VMEM((2, SEG, DH), BF16)
    square = pltpu.VMEM((2, 3, SEG, SEG), BF16)
    terms = pltpu.VMEM((2, 2, SEG, DH), BF16)
    out = jax.ShapeDtypeStruct(query_rows.shape, BF16)
    in_hbm = [pl.BlockSpec(memory_space=pltpu.HBM)] * 4
    parts = pl.pallas_call(
        kernel,
        out_shape=[out] * 4,
        in_specs=in_hbm,
        out_specs=in_hbm,
        scratch_shapes=[
            rows, rows, window, window, pair, pair, square, square, pair,
            pltpu.VMEM((2, SEG, DH), F32), pltpu.VMEM((2, SEG, 1), F32),
            pair, pair, pair, pair, terms, terms,
            dma((4,)), dma((4,)), dma((4,)), dma((4, 2)),
            dma((2, 2)), dma((2, 2)), dma((2, 2)), dma((2, 2)), dma((4,)), dma((4,)),
        ],
        compiler_params=pltpu.CompilerParams(
            collective_id=0, has_side_effects=True, vmem_limit_bytes=63 * 2**20
        ),
        cost_estimate=pl.CostEstimate(flops=2_400_000_000, bytes_accessed=2 * 2**20, transcendentals=1_600_000),
        name="window_attention",
    )(query_rows, key_rows, value_rows, grad_out)
    return pl.pallas_call(
        handover,
        out_shape=[out] * 4,
        in_specs=in_hbm,
        out_specs=in_hbm,
        scratch_shapes=[rows, dma((4,)), dma((4,))],
        compiler_params=pltpu.CompilerParams(vmem_limit_bytes=63 * 2**20),
        name="handover",
    )(*parts)


def solution(mesh):
    spec = P(("blk", "head"), None)
    return jax.shard_map(
        on_device, mesh=mesh, in_specs=(spec,) * 4, out_specs=(spec,) * 4, check_vma=False
    )
```

```python
import math

import jax
import jax.numpy as jnp
from jax import lax
from jax.experimental import pallas as pl
from jax.experimental.pallas import tpu as pltpu
from jax.sharding import PartitionSpec as P

DH = 128
HEADS = 16
SEG = 512
ROWS = 64
Q_ROWS = 256
GRANT = 52 * 2**20 + 7 * 2**17
SCALE = 1.0 / math.sqrt(DH)
SCALE_2 = SCALE * math.log2(math.e)
BF16 = jnp.bfloat16
F32 = jnp.float32
MESH = pl.DeviceIdType.MESH
PLANE = (
    (2, 2), (2, 1), (1, 2), (2, 3), (3, 2), (1, 1), (3, 3), (1, 3), (3, 1),
    (0, 2), (2, 0), (0, 1), (1, 0), (0, 3), (3, 0), (0, 0),
)
OWNERS = ((1, 2), (0, 2), (1, 1), (1, 3), (0, 1), (0, 3), (1, 0), (0, 0))


def nt(lhs, rhs):
    return lax.dot_general(lhs, rhs, (((1,), (1,)), ((), ())), preferred_element_type=F32)


def nn(lhs, rhs):
    return lax.dot_general(lhs, rhs, (((1,), (0,)), ((), ())), preferred_element_type=F32)


def kernel(
    q_in, k_in, v_in, g_in, att_out, dq_out, dk_out, dv_out,
    staged_in, kw, vw, q_s, g_s, e_s, d_s, gp_t, att_f, inv_s, att_st, dq_st, dk_st, dv_st,
    t_send, t_recv, stage_sem,
    in_send, in_recv, halo_send, halo_recv, term_send, term_recv, out_send, out_recv,
):
    head = lax.axis_index("head")
    blk = lax.axis_index("blk")
    planes = lax.axis_size("blk") // 4
    z, y_hi, core = blk // 4, (blk // 2) % 2, blk % 2
    y_lo, x = head // 4, head % 4
    y = 2 * y_hi + y_lo
    mine = 4 * y + x
    away = (y_hi + core) % 2
    at_home = away == 0
    at_end = jnp.where(z + core == 0, 1, 0) + jnp.where(z + core == planes, 1, 0)
    has_far = at_end == 0
    far = {"blk": blk - 3 + 6 * core, "head": head}
    near = {"blk": blk + 1 - 2 * core, "head": head}
    segs = (core, 1 - core)

    def remote(src, dst, send, recv, target):
        pltpu.make_async_remote_copy(
            src_ref=src, dst_ref=dst, send_sem=send, recv_sem=recv, device_id=target, device_id_type=MESH
        ).start()

    def settle(ref, sem):
        pltpu.make_async_copy(ref, ref, sem).wait()

    def owners(turn):
        for dy, dx in OWNERS:
            there = ((y_lo + dy) % 2) * 4 + (x + dx) % 4
            yield {"blk": 4 * z + 2 * core + segs[turn], "head": there}, there, turn == 0 and (dy, dx) == (0, 0)

    inputs, results = (k_in, v_in, q_in, g_in), (att_out, dq_out, dk_out, dv_out)
    staging = [pltpu.make_async_copy(src, staged_in.at[n], stage_sem.at[n]) for n, src in enumerate(inputs)]
    for copy in staging:
        copy.start()
    barrier = pltpu.get_barrier_semaphore()

    def greet(target):
        pl.semaphore_signal(barrier, inc=1, device_id=target, device_id_type=MESH)

    pl.when(has_far)(lambda: greet(far))
    greet(near)
    for turn in range(2):
        for target, _, own in owners(turn):
            if own:
                pl.when(jnp.logical_not(at_home))(lambda target=target: greet(target))
            else:
                greet(target)

    @pl.when(jnp.logical_not(has_far))
    def _():
        kw[3 * core] = jnp.zeros((SEG, DH), BF16)
        vw[3 * core] = jnp.zeros((SEG, DH), BF16)
        t_recv[0, 0] = jnp.zeros((DH, SEG), BF16)
        t_recv[1, 0] = jnp.zeros((DH, SEG), BF16)

    pl.semaphore_wait(barrier, 17 + away - at_end)

    my_rows = pl.ds(pl.multiple_of(head * ROWS, ROWS), ROWS)
    my_column = pl.ds(pl.multiple_of(mine * DH, DH), DH)

    def spread(n, landing):
        send, recv = in_send.at[n], in_recv.at[n, away]
        staging[n].wait()
        for dy, dx in PLANE:
            there_y, there_x = (y + dy) % 4, (x + dx) % 4
            columns = pl.ds(pl.multiple_of((4 * there_y + there_x) * DH, DH), DH)
            target = {"blk": 4 * z + 2 * (there_y // 2) + y_hi, "head": (there_y % 2) * 4 + there_x}

            def go(columns=columns, target=target):
                remote(staged_in.at[n, :, columns], landing, send, recv, target)

            if (dy, dx) == (0, 0):
                pl.when(jnp.logical_not(at_home))(go)

                @pl.when(at_home)
                def _():
                    pltpu.make_async_copy(inputs[n].at[:, my_column], landing, recv).start()
            else:
                go()

    spread(0, kw.at[1 + core, my_rows, :])
    spread(1, vw.at[1 + core, my_rows, :])
    spread(2, q_s.at[away, my_rows, :])
    spread(3, g_s.at[away, my_rows, :])

    for n, window in enumerate((kw, vw)):
        settle(window.at[1 + core], in_recv.at[n, 0])
        pl.when(has_far)(lambda n=n, window=window: remote(
            window.at[1 + core], window.at[3 - 3 * core], halo_send.at[n, 0], halo_recv.at[n, 0], far
        ))
        settle(window.at[2 - core], in_recv.at[n, 1])
        remote(window.at[2 - core], window.at[3 * core], halo_send.at[n, 1], halo_recv.at[n, 1], near)

    def collect(staged, n, turn):
        for target, there, own in owners(turn):
            rows = pl.ds(pl.multiple_of(there * ROWS, ROWS), ROWS)

            def go(rows=rows, target=target):
                remote(staged.at[turn, rows, :], results[n].at[:, my_column], out_send.at[n], out_recv.at[n], target)

            if own:
                pl.when(jnp.logical_not(at_home))(go)

                @pl.when(at_home)
                def _():
                    pltpu.make_async_copy(
                        staged.at[turn, my_rows, :], results[n].at[:, my_column], out_recv.at[n]
                    ).start()
            else:
                go()

    def attend(turn):
        seg = segs[turn]
        inside = (True, True, True)
        if turn == 0:
            inside = (core + (1 - at_end) > 0, True, 1 - core + (1 - at_end) > 0)
        factors = [SCALE_2 if ok is True else jnp.where(ok, SCALE_2, 0.0) for ok in inside]
        for r in range(0, SEG, Q_ROWS):
            rows = pl.ds(r, Q_ROWS)
            query = q_s[turn, rows, :]
            scores = [nt(query, kw[seg + j]) for j in range(3)]
            tops = [jnp.max(s, axis=1, keepdims=True) for s in scores]
            tops = [t if ok is True else jnp.where(ok, t, -jnp.inf) for t, ok in zip(tops, inside)]
            top = jnp.maximum(jnp.maximum(tops[0], tops[1]), tops[2]) * SCALE_2
            total = 0.0
            attended = 0.0
            for j in range(3):
                shift = top if inside[j] is True else jnp.where(inside[j], top, 1e30)
                e = jnp.exp2(scores[j] * factors[j] - shift)
                total = total + jnp.sum(e, axis=1, keepdims=True)
                low = e.astype(BF16)
                e_s[turn, j, rows, :] = low
                attended = attended + nn(low, vw[seg + j])
            inverse = 1.0 / total
            attended = attended * inverse
            att_st[turn, rows, :] = attended.astype(BF16)
            att_f[turn, rows, :] = attended
            inv_s[turn, rows, :] = inverse * SCALE

    def score_grads(turn):
        seg = segs[turn]
        for r in range(0, SEG, Q_ROWS):
            rows = pl.ds(r, Q_ROWS)
            scaled = (g_s[turn, rows, :].astype(F32) * inv_s[turn, rows, :]).astype(BF16)
            gp_t[turn, :, rows] = scaled.T
            delta = jnp.sum(scaled.astype(F32) * att_f[turn, rows, :], axis=1, keepdims=True)
            for j in range(3):
                dprobs = nt(scaled, vw[seg + j])
                d_s[turn, j, rows, :] = (dprobs - delta).astype(BF16) * e_s[turn, j, rows, :]

    def query_grads(turn):
        seg = segs[turn]
        for r in range(0, SEG, Q_ROWS):
            rows = pl.ds(r, Q_ROWS)
            dq_st[turn, rows, :] = sum(nn(d_s[turn, j, rows, :], kw[seg + j]) for j in range(3)).astype(BF16)

    def value_terms(pairs):
        return sum(nn(gp_t[turn], e_s[turn, j]) for turn, j in pairs) * (1.0 / SCALE)

    def key_terms(pairs):
        return sum(nn(q_s[turn].T, d_s[turn, j]) for turn, j in pairs)

    def send_terms(turn):
        outer = (2 * core, 2 - 2 * core)[turn]
        for n, terms in ((1, value_terms), (0, key_terms)):
            t_send[n, turn] = terms([(turn, outer)]).astype(BF16)

            def go(n=n):
                remote(t_send.at[n, turn], t_recv.at[n, turn], term_send.at[n, turn], term_recv.at[n, turn], (far, near)[turn])

            if turn == 0:
                pl.when(has_far)(go)
            else:
                go()

    def finish(turn):
        across = (2 * core, 2 - 2 * core)[turn]
        for n, terms, staged in ((1, value_terms, dv_st), (0, key_terms, dk_st)):
            own = terms([(turn, 1), (1 - turn, across)])

            def arrive(n=n):
                settle(t_recv.at[n, turn], term_recv.at[n, turn])

            if turn == 0:
                pl.when(has_far)(arrive)
            else:
                arrive()
            staged[turn] = (own + t_recv[n, turn].astype(F32)).astype(BF16).T
            collect(staged, 2 + n, turn)

    for turn in (1, 0):
        settle(q_s.at[turn], in_recv.at[2, turn])
        for n, window in enumerate((kw, vw)):
            if turn == 0:
                pl.when(has_far)(lambda n=n, window=window: settle(window.at[3 * core], halo_recv.at[n, 0]))
            else:
                settle(window.at[3 - 3 * core], halo_recv.at[n, 1])
        attend(turn)
        collect(att_st, 0, turn)
    for turn in range(2):
        settle(g_s.at[turn], in_recv.at[3, turn])
        score_grads(turn)
        send_terms(turn)
        query_grads(turn)
        collect(dq_st, 1, turn)
    finish(0)
    finish(1)

    most = pl.ds(0, 15 * DH)

    def sent(n, sem):
        pl.when(at_home)(lambda: settle(staged_in.at[n, :, most], sem))
        pl.when(jnp.logical_not(at_home))(lambda: settle(staged_in.at[n], sem))

    for n in range(4):
        settle(results[n], out_recv.at[n])
        sent(n, in_send.at[n])
        sent(n, out_send.at[n])
    for n in range(2):
        pl.when(has_far)(lambda n=n: settle(kw.at[0], halo_send.at[n, 0]))
        settle(kw.at[0], halo_send.at[n, 1])
        pl.when(has_far)(lambda n=n: settle(t_send.at[n, 0], term_send.at[n, 0]))
        settle(t_send.at[n, 1], term_send.at[n, 1])


def handover(*refs):
    sources, results, sems = refs[:4], refs[4:8], refs[8]
    copies = [pltpu.make_async_copy(src, dst, sems.at[n]) for n, (src, dst) in enumerate(zip(sources, results))]
    for copy in copies:
        copy.start()
    for copy in copies:
        copy.wait()


def on_device(query_rows, key_rows, value_rows, grad_out):
    dma = pltpu.SemaphoreType.DMA
    rows = pltpu.VMEM((4, ROWS, HEADS * DH), BF16)
    window = pltpu.VMEM((4, SEG, DH), BF16)
    pair = pltpu.VMEM((2, SEG, DH), BF16)
    square = pltpu.VMEM((2, 3, SEG, SEG), BF16)
    turned = pltpu.VMEM((2, DH, SEG), BF16)
    terms = pltpu.VMEM((2, 2, DH, SEG), BF16)
    out = jax.ShapeDtypeStruct(query_rows.shape, BF16)
    in_hbm = [pl.BlockSpec(memory_space=pltpu.HBM)] * 4
    parts = pl.pallas_call(
        kernel,
        out_shape=[out] * 4,
        in_specs=in_hbm,
        out_specs=in_hbm,
        scratch_shapes=[
            rows, window, window, pair, pair, square, square, turned,
            pltpu.VMEM((2, SEG, DH), F32), pltpu.VMEM((2, SEG, 1), F32),
            pair, pair, pair, pair, terms, terms,
            dma((4,)), dma((4,)), dma((4, 2)),
            dma((2, 2)), dma((2, 2)), dma((2, 2)), dma((2, 2)), dma((4,)), dma((4,)),
        ],
        compiler_params=pltpu.CompilerParams(
            collective_id=0, has_side_effects=True, vmem_limit_bytes=GRANT
        ),
        cost_estimate=pl.CostEstimate(flops=2_400_000_000, bytes_accessed=2 * 2**20, transcendentals=1_600_000),
        name="window_attention",
    )(query_rows, key_rows, value_rows, grad_out)
    return pl.pallas_call(
        handover,
        out_shape=[out] * 4,
        in_specs=in_hbm,
        out_specs=in_hbm,
        scratch_shapes=[dma((4,))],
        compiler_params=pltpu.CompilerParams(vmem_limit_bytes=GRANT),
        name="handover",
    )(*parts)


def solution(mesh):
    spec = P(("blk", "head"), None)
    return jax.shard_map(
        on_device, mesh=mesh, in_specs=(spec,) * 4, out_specs=(spec,) * 4, check_vma=False
    )
```

```python
import math

import jax
import jax.numpy as jnp
from jax import lax
from jax.experimental import pallas as pl
from jax.experimental.pallas import tpu as pltpu
from jax.sharding import PartitionSpec as P

DH = 128
HEADS = 16
SEG = 512
ROWS = 64
Q_ROWS = 256
GRANT = 52 * 2**20 + 7 * 2**17
SCALE = 1.0 / math.sqrt(DH)
SCALE_2 = SCALE * math.log2(math.e)
BF16 = jnp.bfloat16
F32 = jnp.float32
MESH = pl.DeviceIdType.MESH
PLANE = (
    (2, 2), (2, 1), (1, 2), (2, 3), (3, 2), (1, 1), (3, 3), (1, 3), (3, 1),
    (0, 2), (2, 0), (0, 1), (1, 0), (0, 3), (3, 0), (0, 0),
)
OWNERS = ((1, 2), (0, 2), (1, 1), (1, 3), (0, 1), (0, 3), (1, 0), (0, 0))


def nt(lhs, rhs):
    return lax.dot_general(lhs, rhs, (((1,), (1,)), ((), ())), preferred_element_type=F32)


def nn(lhs, rhs):
    return lax.dot_general(lhs, rhs, (((1,), (0,)), ((), ())), preferred_element_type=F32)


def kernel(
    q_in, k_in, v_in, g_in, att_out, dq_out, dk_out, dv_out,
    kw, vw, q_s, g_s, e_s, d_s, gp_t, att_f, inv_s, att_st, dq_st, dk_st, dv_st,
    t_send, t_recv,
    in_send, in_recv, halo_send, halo_recv, term_send, term_recv, out_send, out_recv,
):
    head = lax.axis_index("head")
    blk = lax.axis_index("blk")
    planes = lax.axis_size("blk") // 4
    z, y_hi, core = blk // 4, (blk // 2) % 2, blk % 2
    y_lo, x = head // 4, head % 4
    y = 2 * y_hi + y_lo
    mine = 4 * y + x
    away = (y_hi + core) % 2
    at_home = away == 0
    at_end = jnp.where(z + core == 0, 1, 0) + jnp.where(z + core == planes, 1, 0)
    has_far = at_end == 0
    far = {"blk": blk - 3 + 6 * core, "head": head}
    near = {"blk": blk + 1 - 2 * core, "head": head}
    segs = (core, 1 - core)

    def remote(src, dst, send, recv, target):
        pltpu.make_async_remote_copy(
            src_ref=src, dst_ref=dst, send_sem=send, recv_sem=recv, device_id=target, device_id_type=MESH
        ).start()

    def settle(ref, sem):
        pltpu.make_async_copy(ref, ref, sem).wait()

    def owners(turn):
        for dy, dx in OWNERS:
            there = ((y_lo + dy) % 2) * 4 + (x + dx) % 4
            yield {"blk": 4 * z + 2 * core + segs[turn], "head": there}, there, turn == 0 and (dy, dx) == (0, 0)

    inputs, results = (k_in, v_in, q_in, g_in), (att_out, dq_out, dk_out, dv_out)
    barrier = pltpu.get_barrier_semaphore()

    def greet(target):
        pl.semaphore_signal(barrier, inc=1, device_id=target, device_id_type=MESH)

    pl.when(has_far)(lambda: greet(far))
    greet(near)
    for turn in range(2):
        for target, _, own in owners(turn):
            if own:
                pl.when(jnp.logical_not(at_home))(lambda target=target: greet(target))
            else:
                greet(target)

    @pl.when(jnp.logical_not(has_far))
    def _():
        kw[3 * core] = jnp.zeros((SEG, DH), BF16)
        vw[3 * core] = jnp.zeros((SEG, DH), BF16)
        t_recv[0, 0] = jnp.zeros((DH, SEG), BF16)
        t_recv[1, 0] = jnp.zeros((DH, SEG), BF16)

    pl.semaphore_wait(barrier, 17 + away - at_end)

    my_rows = pl.ds(pl.multiple_of(head * ROWS, ROWS), ROWS)
    my_column = pl.ds(pl.multiple_of(mine * DH, DH), DH)

    def spread(n, landing):
        send, recv = in_send.at[n], in_recv.at[n, away]
        for dy, dx in PLANE:
            there_y, there_x = (y + dy) % 4, (x + dx) % 4
            columns = pl.ds(pl.multiple_of((4 * there_y + there_x) * DH, DH), DH)
            target = {"blk": 4 * z + 2 * (there_y // 2) + y_hi, "head": (there_y % 2) * 4 + there_x}

            def go(columns=columns, target=target):
                remote(inputs[n].at[:, columns], landing, send, recv, target)

            if (dy, dx) == (0, 0):
                pl.when(jnp.logical_not(at_home))(go)

                @pl.when(at_home)
                def _():
                    pltpu.make_async_copy(inputs[n].at[:, my_column], landing, recv).start()
            else:
                go()

    spread(0, kw.at[1 + core, my_rows, :])
    spread(1, vw.at[1 + core, my_rows, :])
    spread(2, q_s.at[away, my_rows, :])
    spread(3, g_s.at[away, my_rows, :])

    for n, window in enumerate((kw, vw)):
        settle(window.at[1 + core], in_recv.at[n, 0])
        pl.when(has_far)(lambda n=n, window=window: remote(
            window.at[1 + core], window.at[3 - 3 * core], halo_send.at[n, 0], halo_recv.at[n, 0], far
        ))
        settle(window.at[2 - core], in_recv.at[n, 1])
        remote(window.at[2 - core], window.at[3 * core], halo_send.at[n, 1], halo_recv.at[n, 1], near)

    def collect(staged, n, turn):
        for target, there, own in owners(turn):
            rows = pl.ds(pl.multiple_of(there * ROWS, ROWS), ROWS)

            def go(rows=rows, target=target):
                remote(staged.at[turn, rows, :], results[n].at[:, my_column], out_send.at[n], out_recv.at[n], target)

            if own:
                pl.when(jnp.logical_not(at_home))(go)

                @pl.when(at_home)
                def _():
                    pltpu.make_async_copy(
                        staged.at[turn, my_rows, :], results[n].at[:, my_column], out_recv.at[n]
                    ).start()
            else:
                go()

    def attend(turn):
        seg = segs[turn]
        inside = (True, True, True)
        if turn == 0:
            inside = (core + (1 - at_end) > 0, True, 1 - core + (1 - at_end) > 0)
        factors = [SCALE_2 if ok is True else jnp.where(ok, SCALE_2, 0.0) for ok in inside]
        for r in range(0, SEG, Q_ROWS):
            rows = pl.ds(r, Q_ROWS)
            query = q_s[turn, rows, :]
            scores = [nt(query, kw[seg + j]) for j in range(3)]
            tops = [jnp.max(s, axis=1, keepdims=True) for s in scores]
            tops = [t if ok is True else jnp.where(ok, t, -jnp.inf) for t, ok in zip(tops, inside)]
            top = jnp.maximum(jnp.maximum(tops[0], tops[1]), tops[2]) * SCALE_2
            total = 0.0
            attended = 0.0
            for j in range(3):
                shift = top if inside[j] is True else jnp.where(inside[j], top, 1e30)
                e = jnp.exp2(scores[j] * factors[j] - shift)
                total = total + jnp.sum(e, axis=1, keepdims=True)
                low = e.astype(BF16)
                e_s[turn, j, rows, :] = low
                attended = attended + nn(low, vw[seg + j])
            inverse = 1.0 / total
            attended = attended * inverse
            att_st[turn, rows, :] = attended.astype(BF16)
            att_f[turn, rows, :] = attended
            inv_s[turn, rows, :] = inverse * SCALE

    def score_grads(turn):
        seg = segs[turn]
        for r in range(0, SEG, Q_ROWS):
            rows = pl.ds(r, Q_ROWS)
            scaled = (g_s[turn, rows, :].astype(F32) * inv_s[turn, rows, :]).astype(BF16)
            gp_t[turn, :, rows] = scaled.T
            delta = jnp.sum(scaled.astype(F32) * att_f[turn, rows, :], axis=1, keepdims=True)
            for j in range(3):
                dprobs = nt(scaled, vw[seg + j])
                d_s[turn, j, rows, :] = (dprobs - delta).astype(BF16) * e_s[turn, j, rows, :]

    def query_grads(turn):
        seg = segs[turn]
        for r in range(0, SEG, Q_ROWS):
            rows = pl.ds(r, Q_ROWS)
            dq_st[turn, rows, :] = sum(nn(d_s[turn, j, rows, :], kw[seg + j]) for j in range(3)).astype(BF16)

    def value_terms(pairs):
        return sum(nn(gp_t[turn], e_s[turn, j]) for turn, j in pairs) * (1.0 / SCALE)

    def key_terms(pairs):
        return sum(nn(q_s[turn].T, d_s[turn, j]) for turn, j in pairs)

    def send_terms(turn):
        outer = (2 * core, 2 - 2 * core)[turn]
        for n, terms in ((1, value_terms), (0, key_terms)):
            t_send[n, turn] = terms([(turn, outer)]).astype(BF16)

            def go(n=n):
                remote(t_send.at[n, turn], t_recv.at[n, turn], term_send.at[n, turn], term_recv.at[n, turn], (far, near)[turn])

            if turn == 0:
                pl.when(has_far)(go)
            else:
                go()

    def finish(turn):
        across = (2 * core, 2 - 2 * core)[turn]
        for n, terms, staged in ((1, value_terms, dv_st), (0, key_terms, dk_st)):
            own = terms([(turn, 1), (1 - turn, across)])

            def arrive(n=n):
                settle(t_recv.at[n, turn], term_recv.at[n, turn])

            if turn == 0:
                pl.when(has_far)(arrive)
            else:
                arrive()
            staged[turn] = (own + t_recv[n, turn].astype(F32)).astype(BF16).T
            collect(staged, 2 + n, turn)

    for turn in (1, 0):
        settle(q_s.at[turn], in_recv.at[2, turn])
        for n, window in enumerate((kw, vw)):
            if turn == 0:
                pl.when(has_far)(lambda n=n, window=window: settle(window.at[3 * core], halo_recv.at[n, 0]))
            else:
                settle(window.at[3 - 3 * core], halo_recv.at[n, 1])
        attend(turn)
        collect(att_st, 0, turn)
    for turn in range(2):
        settle(g_s.at[turn], in_recv.at[3, turn])
        score_grads(turn)
        query_grads(turn)
        collect(dq_st, 1, turn)
        send_terms(turn)
    finish(0)
    finish(1)

    most = pl.ds(0, 15 * DH)

    def sent(n, sem):
        pl.when(at_home)(lambda: settle(results[n].at[:, most], sem))
        pl.when(jnp.logical_not(at_home))(lambda: settle(results[n], sem))

    for n in range(4):
        settle(results[n], out_recv.at[n])
        sent(n, in_send.at[n])
        sent(n, out_send.at[n])
    for n in range(2):
        pl.when(has_far)(lambda n=n: settle(kw.at[0], halo_send.at[n, 0]))
        settle(kw.at[0], halo_send.at[n, 1])
        pl.when(has_far)(lambda n=n: settle(t_send.at[n, 0], term_send.at[n, 0]))
        settle(t_send.at[n, 1], term_send.at[n, 1])


def handover(*refs):
    sources, results, sems = refs[:4], refs[4:8], refs[8]
    copies = [pltpu.make_async_copy(src, dst, sems.at[n]) for n, (src, dst) in enumerate(zip(sources, results))]
    for copy in copies:
        copy.start()
    for copy in copies:
        copy.wait()


def on_device(query_rows, key_rows, value_rows, grad_out):
    dma = pltpu.SemaphoreType.DMA
    window = pltpu.VMEM((4, SEG, DH), BF16)
    pair = pltpu.VMEM((2, SEG, DH), BF16)
    square = pltpu.VMEM((2, 3, SEG, SEG), BF16)
    turned = pltpu.VMEM((2, DH, SEG), BF16)
    terms = pltpu.VMEM((2, 2, DH, SEG), BF16)
    out = jax.ShapeDtypeStruct(query_rows.shape, BF16)
    in_hbm = [pl.BlockSpec(memory_space=pltpu.HBM)] * 4
    parts = pl.pallas_call(
        kernel,
        out_shape=[out] * 4,
        in_specs=in_hbm,
        out_specs=in_hbm,
        scratch_shapes=[
            window, window, pair, pair, square, square, turned,
            pltpu.VMEM((2, SEG, DH), F32), pltpu.VMEM((2, SEG, 1), F32),
            pair, pair, pair, pair, terms, terms,
            dma((4,)), dma((4, 2)),
            dma((2, 2)), dma((2, 2)), dma((2, 2)), dma((2, 2)), dma((4,)), dma((4,)),
        ],
        compiler_params=pltpu.CompilerParams(
            collective_id=0, has_side_effects=True, vmem_limit_bytes=GRANT
        ),
        cost_estimate=pl.CostEstimate(flops=2_400_000_000, bytes_accessed=2 * 2**20, transcendentals=1_600_000),
        name="window_attention",
    )(query_rows, key_rows, value_rows, grad_out)
    return pl.pallas_call(
        handover,
        out_shape=[out] * 4,
        in_specs=in_hbm,
        out_specs=in_hbm,
        scratch_shapes=[dma((4,))],
        compiler_params=pltpu.CompilerParams(vmem_limit_bytes=GRANT),
        name="handover",
    )(*parts)


def solution(mesh):
    spec = P(("blk", "head"), None)
    return jax.shard_map(
        on_device, mesh=mesh, in_specs=(spec,) * 4, out_specs=(spec,) * 4, check_vma=False
    )
```
